512 devices in a mesh: group: 16 (over z, core), table: 32 (over y, x).
Axes of the slice: x: 4, y: 8, z: 8, core: 2. Of those that a mesh axis runs over, the one named last changes fastest.
Arguments:
- embedded: bfloat16 [65536, 4096], P(('group', 'table')), may hold values from -6 to 6
- ngram_ids: int32 [65536, 4], P(('group', 'table')), may hold values from 0 to 6143, as said below
- counts: int32 [65536], P(('group', 'table')), may hold values from 1 to 4
- slab: bfloat16 [6144, 4096], P('table'), may hold values from -6 to 6
- gain: bfloat16 [4096], replicated, may hold values from 0.099609375 to 1.8984375
- cotangent: bfloat16 [65536, 4096], P(('group', 'table')), may hold values from -6 to 6
Outputs:
- normed: bfloat16 [65536, 4096], P(('group', 'table'))
- grad_slab: float32 [6144, 4096], P('table', 'group')
The draws below stay inside these ranges and needn't reach their ends.
Inputs may be any that keep to these rules, and one draw needn't show every extreme that they name: ngram_ids[t, k] = o * 192 + r names row r of table device o. Among the 512 slots of one device, a quarter of the table devices receive exactly 24 slots, half receive exactly 16 and a quarter exactly 8; which table devices receive most is the same for all devices of one group. Slots past a token's count carry ids as well.
All inputs are finite; a program needn't handle non-finite values.
Results may differ from the reference program's by a relative error of at most 0.0029.
Values may be sent and summed in bfloat16 or wider, within the bound.
No kernel may reach another device: no remote copies, remote signals or barrier semaphores. Data moves between devices by JAX's collectives and lax.ppermute only.
A program may use at most 64 MiB of HBM per device.

```python
import jax
import jax.numpy as jnp
import numpy as np
from jax import lax

D = 4096
NGRAM = 4
TOK_DEV = 128
ROWS_DEV = 192
TOKENS = 65536
VROWS = 6144
N_GROUP = 16
N_TABLE = 32


def draw_ngram_ids(key, part):
    key = jax.random.fold_in(key, 7)
    lookups = TOK_DEV * NGRAM
    share = lookups // N_TABLE
    quarter_width = N_TABLE // 4
    tiers = np.concatenate([np.full(quarter_width, 3 * share // 2), np.full(N_TABLE // 2, share), np.full(N_TABLE - quarter_width - N_TABLE // 2, share // 2)])
    ranks = jnp.asarray(np.repeat(np.arange(N_TABLE), tiers), jnp.int32)
    key_owner, key_sorting, key_row, key_map = jax.random.split(key, 4)
    owner_perm = jax.vmap(lambda sub_key: jax.random.permutation(sub_key, N_TABLE))(jax.random.split(key_owner, N_GROUP))
    owners = owner_perm[:, ranks]
    owners = jnp.broadcast_to(owners[:, None, :], (N_GROUP, N_TABLE, lookups)).reshape(N_GROUP * N_TABLE, lookups)
    orders = jax.vmap(lambda sub_key: jax.random.permutation(sub_key, lookups))(jax.random.split(key_sorting, N_GROUP * N_TABLE))
    owners = jnp.take_along_axis(owners, orders, axis=1)
    row_keys = jax.random.split(key_row, 3)
    local_row = jax.random.randint(row_keys[0], (N_GROUP * N_TABLE, lookups), 0, ROWS_DEV)
    local_row = jnp.minimum(local_row, jax.random.randint(row_keys[1], (N_GROUP * N_TABLE, lookups), 0, ROWS_DEV))
    local_row = jnp.minimum(local_row, jax.random.randint(row_keys[2], (N_GROUP * N_TABLE, lookups), 0, ROWS_DEV))
    row_perm = jax.vmap(lambda sub_key: jax.random.permutation(sub_key, ROWS_DEV))(jax.random.split(key_map, N_TABLE))
    table_row = row_perm[owners, local_row]
    result = owners * ROWS_DEV + table_row
    return result.reshape(TOKENS, NGRAM).astype(jnp.int32)


def with_ends(entries, rng, smallest, largest):
    longest = entries.shape.index(max(entries.shape))
    spots = []
    for shift in (0, 1):
        where = [jax.random.randint(jax.random.fold_in(rng, axis), (), 0, length) for axis, length in enumerate(entries.shape)]
        where[longest] = (where[longest] + shift) % entries.shape[longest]
        spots.append(tuple(where))
    return entries.at[spots[0]].set(smallest).at[spots[1]].set(largest)


def level_of(own_key, dims, shards, low, high):
    level = 1.0
    for position, shards_of in shards:
        heights = jax.random.uniform(jax.random.fold_in(jax.random.fold_in(own_key, 6), position), (shards_of,), jnp.float32, low / len(shards), high / len(shards))
        level = level * jnp.repeat(jnp.exp(heights), dims[position] // shards_of).reshape((-1,) + (1,) * (len(dims) - 1 - position))
    return level


def noise(rng, extent, spread, reach, cuts=(), dtype=jnp.bfloat16):
    entries = spread * jax.random.normal(rng, extent, jnp.float32)
    if cuts:
        entries = entries * level_of(rng, extent, cuts, -0.22, 0.18)
    return jnp.clip(entries, -reach, reach).astype(dtype)


def setup_inputs(seed: int = 0) -> dict:
    key_of = jax.random.split(jax.random.key(seed), 7)
    embedded = noise(key_of[0], (TOKENS, D), 1.0, 6.0, ((0, 512),))
    ngram_ids = draw_ngram_ids(jax.random.fold_in(key_of[6], 71), 0)
    counts = with_ends(jax.random.randint(key_of[2], (TOKENS,), 1, NGRAM + 1), jax.random.fold_in(key_of[2], 1), 1, NGRAM).astype(jnp.int32)
    slab = noise(key_of[3], (VROWS, D), 1.0, 6.0, ((0, 32),))
    gain = jnp.clip(1.0 + 0.18 * jax.random.normal(key_of[4], (D,), jnp.float32), 0.099609375, 1.8984375).astype(jnp.bfloat16)
    cotangent = noise(key_of[5], (TOKENS, D), 1.0, 6.0, ((0, 512),))
    return {"embedded": embedded, "ngram_ids": ngram_ids, "counts": counts, "slab": slab, "gain": gain, "cotangent": cotangent}


def reference(embedded, ngram_ids, counts, slab, gain, cotangent):
    tokens, features = embedded.shape
    ngram = ngram_ids.shape[1]
    block_size = min(1024, tokens)
    blocks = tokens // block_size
    gain_f = gain.astype(jnp.float32)

    def one_block(carry, input_values):
        embedding_block, id_block, count_block, cot_block = input_values
        live = (jnp.arange(ngram)[None, :] < count_block[:, None]).astype(jnp.float32)
        gathered = slab[id_block].astype(jnp.float32) * live[:, :, None]
        count_f = count_block[:, None].astype(jnp.float32)
        pooled = lax.optimization_barrier(jnp.sum(gathered, axis=1)) / count_f
        hidden = embedding_block.astype(jnp.float32) + pooled
        inv_rms = lax.rsqrt(lax.optimization_barrier(jnp.mean(hidden * hidden, axis=-1, keepdims=True)) + 1e-05)
        normed = (hidden * inv_rms * gain_f).astype(jnp.bfloat16)
        grad_out = cot_block.astype(jnp.float32) * gain_f
        inner_term = lax.optimization_barrier(jnp.mean(hidden * grad_out, axis=-1, keepdims=True))
        grad_hidden = inv_rms * grad_out - hidden * (inv_rms * inv_rms * inv_rms) * inner_term
        token_grad = (grad_hidden / count_f).astype(jnp.bfloat16)
        contrib = token_grad.astype(jnp.float32)[:, None, :] * live[:, :, None]
        carry = carry.at[id_block.reshape(-1)].add(contrib.reshape(-1, features))
        return (carry, normed)
    init = jnp.zeros((slab.shape[0], features), jnp.float32)
    grad_slab, normed = lax.scan(one_block, init, (embedded.reshape(blocks, block_size, features), ngram_ids.reshape(blocks, block_size, ngram), counts.reshape(blocks, block_size), cotangent.reshape(blocks, block_size, features)))
    return (normed.reshape(tokens, features), grad_slab)
```

```python
import functools

import jax
import jax.numpy as jnp
from jax import lax
from jax.experimental import pallas as pl
from jax.experimental.pallas import tpu as pltpu
from jax.sharding import Mesh, PartitionSpec as P

Z, C, Y, X = 8, 2, 8, 4
G = ("z", "c")
T = ("y", "x")


def count_kernel(step, wide, a_ref, b_ref, out_ref):
    ngram = max(a_ref.shape[1], b_ref.shape[0])
    rows, cols = out_ref.shape

    def strip(i, carry):
        here = pl.ds(pl.multiple_of(i * step, step), step)
        a = a_ref[here, :]
        for j in range(0, cols, wide):
            b = b_ref[:, j : j + wide]
            total = None
            for k in range(ngram):
                ak = a[:, k : k + 1] if a.shape[1] > 1 else a
                bk = b[k : k + 1, :] if b.shape[0] > 1 else b
                term = jnp.where(ak == bk, 1.0, 0.0)
                total = term if total is None else total + term
            out_ref[here, j : j + wide] = total.astype(jnp.bfloat16)
        return carry

    lax.fori_loop(0, rows // step, strip, 0)


def count_matrix(a, b, block):
    rows, cols = a.shape[0], b.shape[1]
    return pl.pallas_call(
        functools.partial(count_kernel, 32, 512),
        grid=(rows // block,),
        in_specs=[
            pl.BlockSpec((block, a.shape[1]), lambda i: (i, 0)),
            pl.BlockSpec(b.shape, lambda i: (0, 0)),
        ],
        out_specs=pl.BlockSpec((block, cols), lambda i: (i, 0)),
        out_shape=jax.ShapeDtypeStruct((rows, cols), jnp.bfloat16),
        cost_estimate=pl.CostEstimate(
            flops=rows * cols * 12, bytes_accessed=rows * cols * 2, transcendentals=0
        ),
        compiler_params=pltpu.CompilerParams(vmem_limit_bytes=24 * 2**20),
    )(a, b)


def swap_core(v):
    return lax.ppermute(v, "c", [(0, 1), (1, 0)])


def both_cores(v):
    other = swap_core(v)
    first = lax.axis_index("c") == 0
    return jnp.concatenate([jnp.where(first, v, other), jnp.where(first, other, v)], axis=0)


def spread(v, n, axis):
    whole = jnp.broadcast_to(v[None], (n,) + v.shape)
    return lax.all_to_all(whole, axis, split_axis=0, concat_axis=0, tiled=True)


def to_features(v, blocks):
    tok, features = v.shape
    v = v.reshape(tok, blocks, features // blocks).transpose(1, 0, 2)
    v = lax.all_to_all(v, G, split_axis=0, concat_axis=0, tiled=True)
    return v.reshape(blocks * tok, features // blocks)


def per_device(embedded, ngram_ids, counts, slab, gain, cotangent):
    tok, features = embedded.shape
    ngram = ngram_ids.shape[1]
    rows = slab.shape[0]
    blocks = Z * C
    width = features // blocks
    all_rows = rows * Y * X
    all_tok = tok * blocks
    mine = lax.axis_index(G) * width
    here_x = lax.axis_index("x")

    piece = lax.dynamic_slice(slab, (0, mine), (rows, width))
    pieces = [piece] + [
        lax.ppermute(piece, "x", [(i, (i + s) % X) for i in range(X)]) for s in range(1, X)
    ]
    table = lax.all_gather(jnp.concatenate(pieces, axis=0), "y", tiled=True)
    from_x = (here_x - jnp.arange(X)) % X
    owner = jnp.arange(Y)[:, None] * X + from_x[None, :]
    table_row = (owner[:, :, None] * rows + jnp.arange(rows)).reshape(1, all_rows)
    owner = jnp.arange(X)[:, None] + jnp.arange(Y)[None, :] * X
    grad_row = (owner[:, :, None] * rows + jnp.arange(rows)).reshape(all_rows, 1)

    ids = jnp.where(jnp.arange(ngram)[:, None] < counts[None, :], ngram_ids.T, -1)
    ids = spread(both_cores(ids), Z, "z")
    ids = ids.reshape(blocks, ngram, tok).transpose(1, 0, 2).reshape(ngram, all_tok)
    count_f = jnp.sum((ids >= 0).astype(jnp.float32), axis=0)[:, None]
    hot = count_matrix(ids.T, table_row, 256)
    hot_t = count_matrix(grad_row, ids, 768)

    emb = to_features(embedded, blocks).astype(jnp.float32)
    cot = to_features(cotangent, blocks).astype(jnp.float32)
    gain_f = lax.dynamic_slice(gain, (mine,), (width,)).astype(jnp.float32)

    pooled = jnp.dot(hot, table, preferred_element_type=jnp.float32) / count_f
    hidden = emb + pooled
    grad_out = cot * gain_f
    sums = jnp.stack([jnp.sum(hidden * hidden, axis=1), jnp.sum(hidden * grad_out, axis=1)])
    sums = spread(sums.reshape(2 * all_tok // 128, 128), blocks, G)
    sums = jnp.sum(sums.reshape(blocks, 2, all_tok), axis=0) / features
    inv_rms = lax.rsqrt(sums[0] + 1e-05)[:, None]
    inner = sums[1][:, None]
    normed = (hidden * inv_rms * gain_f).astype(jnp.bfloat16)
    grad_hidden = inv_rms * grad_out - hidden * (inv_rms * inv_rms * inv_rms) * inner
    token_grad = (grad_hidden / count_f).astype(jnp.bfloat16)

    partial = jnp.dot(hot_t, token_grad, preferred_element_type=jnp.float32)
    column = lax.psum_scatter(
        partial.astype(jnp.bfloat16), "x", scatter_dimension=0, tiled=True
    )
    back = lax.all_to_all(
        normed.reshape(blocks, tok, width), G, split_axis=0, concat_axis=0, tiled=True
    )
    normed = back.transpose(1, 0, 2).reshape(tok, features)

    column = lax.all_to_all(
        column.reshape(Y, rows, width), "y", split_axis=0, concat_axis=0, tiled=True
    )
    row_grads = jnp.sum(column.astype(jnp.float32), axis=0)
    return (normed, row_grads)


def solution(mesh):
    fine = Mesh(mesh.devices.reshape(Z, C, Y, X), ("z", "c", "y", "x"))
    every = ("z", "c", "y", "x")
    in_specs = (P(every, None), P(every, None), P(every), P(T, None), P(), P(every, None))
    out_specs = (P(every, None), P(T, G))
    return jax.shard_map(
        per_device, mesh=fine, in_specs=in_specs, out_specs=out_specs, check_vma=False
    )
```

```python
import functools

import jax
import jax.numpy as jnp
from jax import lax
from jax.experimental import pallas as pl
from jax.experimental.pallas import tpu as pltpu
from jax.sharding import Mesh, PartitionSpec as P

Z, C, Y, X = 8, 2, 8, 4
G = ("z", "c")
T = ("y", "x")
ROWS_Y = 80


def count_kernel(step, wide, a_ref, b_ref, out_ref):
    ngram = max(a_ref.shape[1], b_ref.shape[0])
    rows, cols = out_ref.shape

    def strip(i, carry):
        here = pl.ds(pl.multiple_of(i * step, step), step)
        a = a_ref[here, :]
        for j in range(0, cols, wide):
            b = b_ref[:, j : j + wide]
            total = None
            for k in range(ngram):
                ak = a[:, k : k + 1] if a.shape[1] > 1 else a
                bk = b[k : k + 1, :] if b.shape[0] > 1 else b
                term = jnp.where(ak == bk, 1.0, 0.0)
                total = term if total is None else total + term
            out_ref[here, j : j + wide] = total.astype(jnp.bfloat16)
        return carry

    lax.fori_loop(0, rows // step, strip, 0)


def count_matrix(a, b, block):
    rows, cols = a.shape[0], b.shape[1]
    return pl.pallas_call(
        functools.partial(count_kernel, 32, 512),
        grid=(rows // block,),
        in_specs=[
            pl.BlockSpec((block, a.shape[1]), lambda i: (i, 0)),
            pl.BlockSpec(b.shape, lambda i: (0, 0)),
        ],
        out_specs=pl.BlockSpec((block, cols), lambda i: (i, 0)),
        out_shape=jax.ShapeDtypeStruct((rows, cols), jnp.bfloat16),
        cost_estimate=pl.CostEstimate(
            flops=rows * cols * 12, bytes_accessed=rows * cols * 2, transcendentals=0
        ),
        compiler_params=pltpu.CompilerParams(vmem_limit_bytes=24 * 2**20),
    )(a, b)


def shift(s):
    return [(i, (i + s) % X) for i in range(X)]


def spread(v, n, axis):
    whole = jnp.broadcast_to(v[None], (n,) + v.shape)
    return lax.all_to_all(whole, axis, split_axis=0, concat_axis=0, tiled=True)


def two_runs(v):
    late = v[:, :, ROWS_Y:].transpose(1, 0, 2, 3)
    return v[:, :, :ROWS_Y].reshape(-1, v.shape[3]), late.reshape(-1, v.shape[3])


def rows_of(hot, token_grad):
    return lax.dot_general(
        hot, token_grad, (((0,), (0,)), ((), ())), preferred_element_type=jnp.float32
    )


def per_device(embedded, ngram_ids, counts, slab, gain, cotangent):
    tok, features = embedded.shape
    ngram = ngram_ids.shape[1]
    rows = slab.shape[0]
    blocks = Z * C
    width = features // blocks
    all_rows = rows * Y * X
    all_tok = tok * blocks
    mine = lax.axis_index(G) * width
    here_x = lax.axis_index("x")

    ids = jnp.where(jnp.arange(ngram)[:, None] < counts[None, :], ngram_ids.T, -1)
    ids = spread(ids, blocks, G)
    ids, embedded, cotangent = lax.optimization_barrier((ids, embedded, cotangent))
    ids = ids.transpose(0, 2, 1).reshape(all_tok, ngram)

    sent = jnp.concatenate([embedded, cotangent], axis=0)
    sent = sent.reshape(2 * tok, blocks, width).transpose(1, 0, 2)
    came = lax.all_to_all(sent, G, split_axis=0, concat_axis=0, tiled=True)

    piece = lax.dynamic_slice(slab, (0, mine), (rows, width))
    pieces = [piece] + [lax.ppermute(piece, "x", shift(s)) for s in range(1, X)]
    table = lax.all_gather(jnp.concatenate(pieces, axis=0), "y", tiled=True)
    from_x = (here_x - jnp.arange(X)) % X
    owner = jnp.arange(Y)[:, None] * X + from_x[None, :]
    table_row = owner[:, :, None] * rows + jnp.arange(rows)
    table_y, table_x = two_runs(table.reshape(Y, X, rows, width))
    row_y, row_x = two_runs(table_row[..., None])

    count_f = jnp.sum((ids >= 0).astype(jnp.float32), axis=1, keepdims=True)
    hot_x = count_matrix(ids, row_x.T, 256)
    hot_x, ids = lax.optimization_barrier((hot_x, ids))
    hot_y = count_matrix(ids, row_y.T, 256)

    gain_f = lax.dynamic_slice(gain, (mine,), (width,)).astype(jnp.float32)

    pooled = jnp.dot(hot_x, table_x, preferred_element_type=jnp.float32)
    pooled = pooled + jnp.dot(hot_y, table_y, preferred_element_type=jnp.float32)
    pooled, came = lax.optimization_barrier((pooled, came))
    emb = came[:, :tok].reshape(all_tok, width).astype(jnp.float32)
    cot = came[:, tok:].reshape(all_tok, width).astype(jnp.float32)
    hidden = emb + pooled / count_f
    grad_out = cot * gain_f
    sums = jnp.stack([jnp.sum(hidden * hidden, axis=1), jnp.sum(hidden * grad_out, axis=1)])
    sums = spread(sums.reshape(2 * all_tok // 128, 128), blocks, G)
    sums = jnp.sum(sums.reshape(blocks, 2, all_tok), axis=0) / features
    inv_rms = lax.rsqrt(sums[0] + 1e-05)[:, None]
    inner = sums[1][:, None]
    normed = (hidden * inv_rms * gain_f).astype(jnp.bfloat16)
    grad_hidden = inv_rms * grad_out - hidden * (inv_rms * inv_rms * inv_rms) * inner
    token_grad = lax.optimization_barrier((grad_hidden / count_f).astype(jnp.bfloat16))

    by_y = rows_of(hot_y, token_grad)
    by_y, token_grad = lax.optimization_barrier((by_y, token_grad))
    by_y = lax.psum_scatter(by_y, "y", scatter_dimension=0, tiled=True)

    run = Y * (rows - ROWS_Y)
    by_x = []
    for s in (2, 1, 3, 0):
        part = rows_of(hot_x[:, s * run : (s + 1) * run], token_grad)
        if s:
            part = part.astype(jnp.bfloat16)
        part, token_grad = lax.optimization_barrier((part, token_grad))
        if s:
            part = lax.ppermute(part, "x", shift(-s)).astype(jnp.float32)
        by_x.append(part)
    by_x = sum(by_x[::-1]).astype(jnp.bfloat16).reshape(Y, rows - ROWS_Y, width)

    back = lax.all_to_all(
        normed.reshape(blocks, tok, width), G, split_axis=0, concat_axis=0, tiled=True
    )

    by_x, back = lax.optimization_barrier((by_x, back))
    normed = back.transpose(1, 0, 2).reshape(tok, features)
    by_x = lax.all_to_all(by_x, "y", split_axis=0, concat_axis=0, tiled=True)
    by_x = jnp.sum(by_x.astype(jnp.float32), axis=0)
    by_y = by_y.reshape(X, ROWS_Y, width)
    by_y = by_y[0] + sum(lax.ppermute(by_y[s], "x", shift(-s)) for s in range(1, X))
    row_grads = jnp.concatenate([by_y, by_x], axis=0)
    return (normed, row_grads)


def solution(mesh):
    fine = Mesh(mesh.devices.reshape(Z, C, Y, X), ("z", "c", "y", "x"))
    every = ("z", "c", "y", "x")
    in_specs = (P(every, None), P(every, None), P(every), P(T, None), P(), P(every, None))
    out_specs = (P(every, None), P(T, G))
    return jax.shard_map(
        per_device, mesh=fine, in_specs=in_specs, out_specs=out_specs, check_vma=False
    )
```

```python
import functools

import jax
import jax.numpy as jnp
from jax import lax
from jax.experimental import pallas as pl
from jax.experimental.pallas import tpu as pltpu
from jax.sharding import Mesh, PartitionSpec as P

Z, C, Y, X = 8, 2, 8, 4
G = ("z", "c")
T = ("y", "x")
ROWS_Y = 80


def count_kernel(step, wide, a_ref, b_ref, out_ref):
    rows, cols = out_ref.shape
    one = jnp.ones((step, wide), jnp.bfloat16)
    zero = jnp.zeros((step, wide), jnp.bfloat16)

    def strip(i, carry):
        here = pl.ds(pl.multiple_of(i * step, step), step)
        a = a_ref[here, :]
        a = [
            jnp.broadcast_to(a[:, k : k + 1], (step, wide)).astype(jnp.int16)
            for k in range(a.shape[1])
        ]
        for j in range(0, cols, wide):
            b = b_ref[:, j : j + wide]
            terms = [jnp.where(ak == b, one, zero) for ak in a]
            out_ref[here, j : j + wide] = (terms[0] + terms[1]) + (terms[2] + terms[3])
        return carry

    lax.fori_loop(0, rows // step, strip, 0)


def count_matrix(a, b, block):
    rows, cols, step = a.shape[0], b.shape[0], 32
    b = jnp.broadcast_to(b.astype(jnp.int16)[None, :], (step, cols))
    return pl.pallas_call(
        functools.partial(count_kernel, step, 256),
        grid=(rows // block,),
        in_specs=[
            pl.BlockSpec((block, a.shape[1]), lambda i: (i, 0)),
            pl.BlockSpec(b.shape, lambda i: (0, 0)),
        ],
        out_specs=pl.BlockSpec((block, cols), lambda i: (i, 0)),
        out_shape=jax.ShapeDtypeStruct((rows, cols), jnp.bfloat16),
        cost_estimate=pl.CostEstimate(
            flops=rows * cols * 12, bytes_accessed=rows * cols * 2, transcendentals=0
        ),
        compiler_params=pltpu.CompilerParams(vmem_limit_bytes=60 * 2**20),
    )(a, b)


def pool_kernel(hot_ref, table_ref, out_ref):
    out_ref[...] = jnp.dot(hot_ref[...], table_ref[...], preferred_element_type=jnp.float32)


def pool(hot, table, block):
    tok, span = hot.shape
    width = table.shape[1]
    return pl.pallas_call(
        pool_kernel,
        grid=(tok // block,),
        in_specs=[
            pl.BlockSpec((block, span), lambda i: (i, 0)),
            pl.BlockSpec((span, width), lambda i: (0, 0)),
        ],
        out_specs=pl.BlockSpec((block, width), lambda i: (i, 0)),
        out_shape=jax.ShapeDtypeStruct((tok, width), jnp.float32),
        cost_estimate=pl.CostEstimate(
            flops=2 * tok * width * span,
            bytes_accessed=2 * (tok + width) * span + 4 * tok * width,
            transcendentals=0,
        ),
        compiler_params=pltpu.CompilerParams(vmem_limit_bytes=60 * 2**20),
    )(hot, table)


def rows_kernel(hot_ref, grad_ref, by_y_ref, *by_x_refs):
    out = lax.dot_general(
        hot_ref[...],
        grad_ref[...],
        (((0,), (0,)), ((), ())),
        preferred_element_type=jnp.float32,
    )
    out = out.reshape(X, out.shape[0] // X, out.shape[1])
    by_y_ref[0] = out[:, :ROWS_Y]
    for s, ref in enumerate(by_x_refs):
        ref[0] = out[s, ROWS_Y:].astype(ref.dtype)


def rows_of(hot, token_grad, rows):
    tok, width = token_grad.shape
    span = hot.shape[1]
    late = rows - ROWS_Y
    return pl.pallas_call(
        rows_kernel,
        grid=(Y,),
        in_specs=[
            pl.BlockSpec((tok, span // Y), lambda i: (0, i)),
            pl.BlockSpec((tok, width), lambda i: (0, 0)),
        ],
        out_specs=[pl.BlockSpec((1, X, ROWS_Y, width), lambda i: (i, 0, 0, 0))]
        + [pl.BlockSpec((1, late, width), lambda i: (i, 0, 0))] * X,
        out_shape=[jax.ShapeDtypeStruct((Y, X, ROWS_Y, width), jnp.float32)]
        + [
            jax.ShapeDtypeStruct((Y, late, width), jnp.bfloat16 if s else jnp.float32)
            for s in range(X)
        ],
        cost_estimate=pl.CostEstimate(
            flops=2 * tok * width * span,
            bytes_accessed=2 * tok * (span + width) + 4 * span * width,
            transcendentals=0,
        ),
        compiler_params=pltpu.CompilerParams(vmem_limit_bytes=60 * 2**20),
    )(hot, token_grad)


def shift(s):
    return [(i, (i + s) % X) for i in range(X)]


def spread(v, n, axis):
    whole = jnp.broadcast_to(v[None], (n,) + v.shape)
    return lax.all_to_all(whole, axis, split_axis=0, concat_axis=0, tiled=True)


def per_device(embedded, ngram_ids, counts, slab, gain, cotangent):
    tok, features = embedded.shape
    ngram = ngram_ids.shape[1]
    rows = slab.shape[0]
    blocks = Z * C
    width = features // blocks
    all_rows = rows * Y * X
    all_tok = tok * blocks
    mine = lax.axis_index(G) * width
    here_x = lax.axis_index("x")

    ids = jnp.where(jnp.arange(ngram)[:, None] < counts[None, :], ngram_ids.T, -1)
    ids = spread(ids, blocks, G)

    sent = jnp.concatenate([embedded, cotangent], axis=0)
    sent = sent.reshape(2 * tok, blocks, width).transpose(1, 0, 2)
    ids, sent = lax.optimization_barrier((ids, sent))
    came = lax.all_to_all(sent, G, split_axis=0, concat_axis=0, tiled=True)
    ids = ids.transpose(0, 2, 1).reshape(all_tok, ngram)

    piece = lax.dynamic_slice(slab, (0, mine), (rows, width))
    pieces = [piece] + [lax.ppermute(piece, "x", shift(s)) for s in range(1, X)]
    table = lax.all_gather(jnp.concatenate(pieces, axis=0), "y", tiled=True)
    owner = jnp.arange(Y)[:, None] * X + (here_x - jnp.arange(X)) % X
    table_row = (owner[:, :, None] * rows + jnp.arange(rows)).reshape(all_rows)

    count_f = jnp.sum((ids >= 0).astype(jnp.float32), axis=1, keepdims=True)
    hot = count_matrix(ids, table_row, 256)

    gain_f = lax.dynamic_slice(gain, (mine,), (width,)).astype(jnp.float32)

    pooled = pool(hot, table, 256)
    pooled, came = lax.optimization_barrier((pooled, came))
    emb = came[:, :tok].reshape(all_tok, width).astype(jnp.float32)
    cot = came[:, tok:].reshape(all_tok, width).astype(jnp.float32)
    hidden = emb + pooled / count_f
    grad_out = cot * gain_f
    sums = jnp.stack([jnp.sum(hidden * hidden, axis=1), jnp.sum(hidden * grad_out, axis=1)])
    sums = spread(sums.reshape(2 * all_tok // 128, 128), blocks, G)
    sums = jnp.sum(sums.reshape(blocks, 2, all_tok), axis=0) / features
    inv_rms = lax.rsqrt(sums[0] + 1e-05)[:, None]
    inner = sums[1][:, None]
    normed = (hidden * inv_rms * gain_f).astype(jnp.bfloat16)
    grad_hidden = inv_rms * grad_out - hidden * (inv_rms * inv_rms * inv_rms) * inner
    token_grad = lax.optimization_barrier((grad_hidden / count_f).astype(jnp.bfloat16))

    by_y, *by_x = rows_of(hot, token_grad, rows)
    by_y = lax.psum_scatter(
        by_y.reshape(Y * X * ROWS_Y, width), "y", scatter_dimension=0, tiled=True
    )
    by_x = [by_x[0]] + [lax.ppermute(by_x[s], "x", shift(-s)) for s in (2, 1, 3)]
    by_x = sum(v.astype(jnp.float32) for v in by_x).astype(jnp.bfloat16)

    back = lax.all_to_all(
        normed.reshape(blocks, tok, width), G, split_axis=0, concat_axis=0, tiled=True
    )

    by_x, back = lax.optimization_barrier((by_x, back))
    normed = back.transpose(1, 0, 2).reshape(tok, features)
    by_x = lax.all_to_all(by_x, "y", split_axis=0, concat_axis=0, tiled=True)
    by_x = jnp.sum(by_x.astype(jnp.float32), axis=0)
    by_y = by_y.reshape(X, ROWS_Y, width)
    by_y = by_y[0] + sum(lax.ppermute(by_y[s], "x", shift(-s)) for s in range(1, X))
    row_grads = jnp.concatenate([by_y, by_x], axis=0)
    return (normed, row_grads)


def solution(mesh):
    fine = Mesh(mesh.devices.reshape(Z, C, Y, X), ("z", "c", "y", "x"))
    every = ("z", "c", "y", "x")
    in_specs = (P(every, None), P(every, None), P(every), P(T, None), P(), P(every, None))
    out_specs = (P(every, None), P(T, G))
    return jax.shard_map(
        per_device, mesh=fine, in_specs=in_specs, out_specs=out_specs, check_vma=False
    )
```

```python
import functools

import jax
import jax.numpy as jnp
from jax import lax
from jax.experimental import pallas as pl
from jax.experimental.pallas import tpu as pltpu
from jax.sharding import Mesh, PartitionSpec as P

Z, C, Y, X = 8, 2, 8, 4
G = ("z", "c")
T = ("y", "x")
ROWS_Y = 80


def count_kernel(step, wide, a_ref, b_ref, out_ref):
    rows, cols = out_ref.shape
    one = jnp.ones((step, wide), jnp.bfloat16)
    zero = jnp.zeros((step, wide), jnp.bfloat16)

    def strip(i, carry):
        here = pl.ds(pl.multiple_of(i * step, step), step)
        a = a_ref[here, :]
        a = [
            jnp.broadcast_to(a[:, k : k + 1], (step, wide)).astype(jnp.int16)
            for k in range(a.shape[1])
        ]
        for j in range(0, cols, wide):
            b = b_ref[:, j : j + wide]
            terms = [jnp.where(ak == b, one, zero) for ak in a]
            out_ref[here, j : j + wide] = (terms[0] + terms[1]) + (terms[2] + terms[3])
        return carry

    lax.fori_loop(0, rows // step, strip, 0)


def count_matrix(a, b, block):
    rows, cols, step = a.shape[0], b.shape[0], 32
    b = jnp.broadcast_to(b.astype(jnp.int16)[None, :], (step, cols))
    return pl.pallas_call(
        functools.partial(count_kernel, step, 256),
        grid=(rows // block,),
        in_specs=[
            pl.BlockSpec((block, a.shape[1]), lambda i: (i, 0)),
            pl.BlockSpec(b.shape, lambda i: (0, 0)),
        ],
        out_specs=pl.BlockSpec((block, cols), lambda i: (i, 0)),
        out_shape=jax.ShapeDtypeStruct((rows, cols), jnp.bfloat16),
        cost_estimate=pl.CostEstimate(
            flops=rows * cols * 12, bytes_accessed=rows * cols * 2, transcendentals=0
        ),
        compiler_params=pltpu.CompilerParams(vmem_limit_bytes=60 * 2**20),
    )(a, b)


def pool_kernel(hot_ref, table_ref, out_ref):
    out_ref[...] = jnp.dot(hot_ref[...], table_ref[...], preferred_element_type=jnp.float32)


def pool(hot, table, block):
    tok, span = hot.shape
    width = table.shape[1]
    return pl.pallas_call(
        pool_kernel,
        grid=(tok // block,),
        in_specs=[
            pl.BlockSpec((block, span), lambda i: (i, 0)),
            pl.BlockSpec((span, width), lambda i: (0, 0)),
        ],
        out_specs=pl.BlockSpec((block, width), lambda i: (i, 0)),
        out_shape=jax.ShapeDtypeStruct((tok, width), jnp.float32),
        cost_estimate=pl.CostEstimate(
            flops=2 * tok * width * span,
            bytes_accessed=2 * (tok + width) * span + 4 * tok * width,
            transcendentals=0,
        ),
        compiler_params=pltpu.CompilerParams(vmem_limit_bytes=60 * 2**20),
    )(hot, table)


def rows_kernel(
    hot_ref, hidden_ref, cot_ref, scales_ref, gain_ref, normed_ref, by_y_ref, *rest
):
    by_x_refs, grad_ref = rest[:-1], rest[-1]
    all_tok, width = cot_ref.shape
    tok = 128
    blocks = all_tok // tok

    @pl.when(pl.program_id(0) == 0)
    def _():
        gain_f = gain_ref[...]
        for b in range(blocks):
            here = pl.ds(b * tok, tok)
            scales = scales_ref[:, here].T
            inv_rms, pull, count = scales[:, 0:1], scales[:, 1:2], scales[:, 2:3]
            hidden = hidden_ref[here, :]
            grad_out = cot_ref[here, :].astype(jnp.float32) * gain_f
            normed_ref[here, :] = (hidden * inv_rms * gain_f).astype(normed_ref.dtype)
            grad_hidden = inv_rms * grad_out - hidden * pull
            grad_ref[here, :] = (grad_hidden / count).astype(grad_ref.dtype)

    out = lax.dot_general(
        hot_ref[...],
        grad_ref[...],
        (((0,), (0,)), ((), ())),
        preferred_element_type=jnp.float32,
    )
    out = out.reshape(X, out.shape[0] // X, out.shape[1])
    by_y_ref[0] = out[:, :ROWS_Y]
    for s, ref in enumerate(by_x_refs):
        ref[0] = out[s, ROWS_Y:].astype(ref.dtype)


def rows_of(hot, hidden, cot, scales, gain_f, rows):
    width = cot.shape[1]
    all_tok, span = hot.shape
    late = rows - ROWS_Y
    return pl.pallas_call(
        rows_kernel,
        grid=(Y,),
        in_specs=[
            pl.BlockSpec((all_tok, span // Y), lambda i: (0, i)),
            pl.BlockSpec((all_tok, width), lambda i: (0, 0)),
            pl.BlockSpec((all_tok, width), lambda i: (0, 0)),
            pl.BlockSpec(scales.shape, lambda i: (0, 0)),
            pl.BlockSpec((1, width), lambda i: (0, 0)),
        ],
        out_specs=[
            pl.BlockSpec((all_tok, width), lambda i: (0, 0)),
            pl.BlockSpec((1, X, ROWS_Y, width), lambda i: (i, 0, 0, 0)),
        ]
        + [pl.BlockSpec((1, late, width), lambda i: (i, 0, 0))] * X,
        out_shape=[
            jax.ShapeDtypeStruct((all_tok, width), jnp.bfloat16),
            jax.ShapeDtypeStruct((Y, X, ROWS_Y, width), jnp.float32),
        ]
        + [
            jax.ShapeDtypeStruct((Y, late, width), jnp.bfloat16 if s else jnp.float32)
            for s in range(X)
        ],
        scratch_shapes=[pltpu.VMEM((all_tok, width), jnp.bfloat16)],
        cost_estimate=pl.CostEstimate(
            flops=2 * all_tok * width * span,
            bytes_accessed=2 * all_tok * (span + 4 * width) + 4 * span * width,
            transcendentals=0,
        ),
        compiler_params=pltpu.CompilerParams(vmem_limit_bytes=60 * 2**20),
    )(hot, hidden, cot, scales, gain_f)


def shift(s):
    return [(i, (i + s) % X) for i in range(X)]


def spread(v, n, axis):
    whole = jnp.broadcast_to(v[None], (n,) + v.shape)
    return lax.all_to_all(whole, axis, split_axis=0, concat_axis=0, tiled=True)


def per_device(embedded, ngram_ids, counts, slab, gain, cotangent):
    tok, features = embedded.shape
    ngram = ngram_ids.shape[1]
    rows = slab.shape[0]
    blocks = Z * C
    width = features // blocks
    all_rows = rows * Y * X
    all_tok = tok * blocks
    mine = lax.axis_index(G) * width
    here_x = lax.axis_index("x")

    ids = jnp.where(jnp.arange(ngram)[:, None] < counts[None, :], ngram_ids.T, -1)
    ids = spread(ids, blocks, G)

    sent = jnp.concatenate([embedded, cotangent], axis=0)
    sent = sent.reshape(2 * tok, blocks, width).transpose(1, 0, 2)
    ids, sent = lax.optimization_barrier((ids, sent))
    came = lax.all_to_all(sent, G, split_axis=0, concat_axis=0, tiled=True)
    ids = ids.transpose(0, 2, 1).reshape(all_tok, ngram)

    piece = lax.dynamic_slice(slab, (0, mine), (rows, width))
    pieces = [piece] + [lax.ppermute(piece, "x", shift(s)) for s in range(1, X)]
    table = lax.all_gather(jnp.concatenate(pieces, axis=0), "y", tiled=True)
    owner = jnp.arange(Y)[:, None] * X + (here_x - jnp.arange(X)) % X
    table_row = (owner[:, :, None] * rows + jnp.arange(rows)).reshape(all_rows)

    hot = count_matrix(ids, table_row, 256)

    gain_f = lax.dynamic_slice(gain, (mine,), (width,)).astype(jnp.float32)
    gain_f = gain_f.reshape(1, width)
    count_f = jnp.sum((ids >= 0).astype(jnp.float32), axis=1)

    pooled = pool(hot, table, 256)
    pooled, came = lax.optimization_barrier((pooled, came))
    emb = came[:, :tok].reshape(all_tok, width).astype(jnp.float32)
    cot = came[:, tok:].reshape(all_tok, width)
    hidden = emb + pooled / count_f[:, None]
    grad_out = cot.astype(jnp.float32) * gain_f
    sums = jnp.stack([jnp.sum(hidden * hidden, axis=1), jnp.sum(hidden * grad_out, axis=1)])
    sums = spread(sums.reshape(2 * all_tok // 128, 128), blocks, G)
    sums = jnp.sum(sums.reshape(blocks, 2, all_tok), axis=0) / features
    inv_rms = lax.rsqrt(sums[0] + 1e-05)
    pull = inv_rms * inv_rms * inv_rms * sums[1]
    scales = jnp.pad(jnp.stack([inv_rms, pull, count_f]), ((0, 5), (0, 0)))
    normed, by_y, *by_x = rows_of(hot, hidden, cot, scales, gain_f, rows)

    by_y = lax.psum_scatter(
        by_y.reshape(Y * X * ROWS_Y, width), "y", scatter_dimension=0, tiled=True
    )
    by_x = [by_x[0]] + [lax.ppermute(by_x[s], "x", shift(-s)) for s in (2, 1, 3)]
    by_x = sum(v.astype(jnp.float32) for v in by_x).astype(jnp.bfloat16)

    back = lax.all_to_all(normed.reshape(blocks, tok, width), G, split_axis=0, concat_axis=0, tiled=True)

    by_x, back = lax.optimization_barrier((by_x, back))
    normed = back.transpose(1, 0, 2).reshape(tok, features)
    by_x = lax.all_to_all(by_x, "y", split_axis=0, concat_axis=0, tiled=True)
    by_x = jnp.sum(by_x.astype(jnp.float32), axis=0)
    by_y = by_y.reshape(X, ROWS_Y, width)
    by_y = by_y[0] + sum(lax.ppermute(by_y[s], "x", shift(-s)) for s in range(1, X))
    row_grads = jnp.concatenate([by_y, by_x], axis=0)
    return (normed, row_grads)


def solution(mesh):
    fine = Mesh(mesh.devices.reshape(Z, C, Y, X), ("z", "c", "y", "x"))
    every = ("z", "c", "y", "x")
    in_specs = (P(every, None), P(every, None), P(every), P(T, None), P(), P(every, None))
    out_specs = (P(every, None), P(T, G))
    return jax.shard_map(
        per_device, mesh=fine, in_specs=in_specs, out_specs=out_specs, check_vma=False
    )
```
